32 devices in a mesh: gx: 8 (over z, x), gy: 4 (over y, core).
Axes of the slice: x: 2, y: 2, z: 4, core: 2. Of those that a mesh axis runs over, the one named last changes fastest.
Arguments:
- fields: float32 [5, 3, 1024, 2048], P(None, None, 'gx', 'gy'), may hold values from -6 to 6
- metric_first: float32 [1024], P('gx'), may hold values from 0.5 to 2
- metric_second: float32 [2048], P('gy'), may hold values from 0.5 to 2
Outputs:
- slope_first: float32 [5, 3, 1024, 2048], P(None, None, 'gx', 'gy')
- slope_second: float32 [5, 3, 1024, 2048], P(None, None, 'gx', 'gy')
The draws below stay inside these ranges and needn't reach their ends.
All inputs are finite; a program needn't handle non-finite values.
Results may differ from the reference program's by a relative error of at most 0.00007.
Values sent between devices are 32-bit elements; how exact they have to be, the bound alone decides.
A program may use at most 128 MiB of HBM per device.

```python
import math
import jax
import jax.numpy as jnp
from jax import lax

FIELDS = 5
PLANES = 3
NX = 1024
NY = 2048


def block_levels(key, shape, pieces, low, high):
    def one(axis_at, parts):
        draws = jax.random.uniform(jax.random.fold_in(jax.random.fold_in(key, 6), axis_at), (parts,), jnp.float32, low / len(pieces), high / len(pieces))
        return jnp.repeat(jnp.exp(draws), shape[axis_at] // parts).reshape((-1,) + (1,) * (len(shape) - axis_at - 1))

    factor_of = one(*pieces[0])
    for cut in pieces[1:]:
        factor_of = factor_of * one(*cut)
    return factor_of


def normal_values(own_key, shape, scale, most, pieces=(), held_as=jnp.bfloat16):
    gain = block_levels(own_key, shape, pieces, -0.22, 0.18) if pieces else 1.0
    values = jax.random.normal(own_key, shape, jnp.float32) * scale * gain
    return jnp.minimum(jnp.maximum(values, -most), most).astype(held_as)


def setup_inputs(seed: int = 0) -> dict:
    arg_keys = jax.random.split(jax.random.key(seed), 4)
    fields = normal_values(arg_keys[0], (FIELDS, PLANES, NX, NY), 1.0, 6.0, ((2, 8), (3, 4)), jnp.float32)
    metric_first = jnp.clip(jnp.exp(math.log(2.0) - 1.3862944 * jax.random.uniform(arg_keys[1], (NX,), jnp.float32) ** block_levels(arg_keys[1], (NX,), ((0, 8),), -0.2, 0.2)), 0.5, 2.0)
    metric_second = jnp.clip(jnp.exp(math.log(2.0) - 1.3862944 * jax.random.uniform(arg_keys[2], (NY,), jnp.float32) ** block_levels(arg_keys[2], (NY,), ((0, 4),), -0.2, 0.2)), 0.5, 2.0)
    return dict(fields=fields, metric_first=metric_first, metric_second=metric_second)


ALPHA = 0.47
COEF_A = 2.0 * (ALPHA + 2.0) / 3.0
COEF_B = (4.0 * ALPHA - 1.0) / 3.0


def explicit_side(values, axis):
    return (COEF_A / 2.0) * (jnp.roll(values, -1, axis) - jnp.roll(values, 1, axis)) + (COEF_B / 4.0) * (jnp.roll(values, -2, axis) - jnp.roll(values, 2, axis))


def periodic_solve(forcing, axis):
    length = forcing.shape[axis]
    wave = jnp.arange(length, dtype=jnp.float32) * (2.0 * jnp.pi / length)
    symbol = 1.0 + 2.0 * ALPHA * jnp.cos(wave)
    profile = [1] * forcing.ndim
    profile[axis] = length
    spectrum = jnp.fft.fft(forcing, axis=axis) / symbol.reshape(profile)
    return jnp.real(jnp.fft.ifft(spectrum, axis=axis)).astype(forcing.dtype)


def reference(fields, metric_first, metric_second):
    def per_field(single):
        compact_first = periodic_solve(explicit_side(single, 1), 1)
        compact_second = periodic_solve(explicit_side(single, 2), 2)
        return compact_first * metric_first[None, :, None], compact_second * metric_second[None, None, :]

    slope_first, slope_second = lax.map(per_field, fields)
    return slope_first, slope_second
```

```python
import jax
import jax.numpy as jnp
import ml_dtypes
import numpy as np
from jax import lax
from jax.experimental import pallas as pl
from jax.experimental.pallas import tpu as pltpu
from jax.sharding import PartitionSpec as P

ALPHA = 0.47
HALF_A = (ALPHA + 2.0) / 3.0
QUARTER_B = (4.0 * ALPHA - 1.0) / 12.0

ROOT = (-1.0 + np.sqrt(1.0 - 4.0 * ALPHA * ALPHA)) / (2.0 * ALPHA)
GAIN = 1.0 / (1.0 + 2.0 * ALPHA * ROOT)
KAPPA = GAIN * (HALF_A * (ROOT - 1.0 / ROOT) + QUARTER_B * (ROOT**2 - ROOT**-2))
DELTA = GAIN * QUARTER_B * (1.0 / ROOT - ROOT)

HIGHEST = lax.Precision.HIGHEST
MIB = 1 << 20


def piece_matrix(extent):
    place = np.arange(extent)
    gap = place[:, None] - place[None, :]
    size = np.abs(gap)
    whole = np.sign(gap) * (KAPPA * ROOT**size + np.where(size == 1, DELTA, 0.0))
    high = whole.astype(ml_dtypes.bfloat16)
    low = (whole - high.astype(np.float64)).astype(ml_dtypes.bfloat16)
    return high, low


def sum_weights(extent):
    place = np.arange(extent)
    rows = np.zeros((8, extent))
    rows[0] = ROOT ** (extent - place)
    rows[1] = ROOT ** (place + 1)
    rows[2, -1] = 1.0
    rows[3, 0] = 1.0
    return rows.astype(np.float32)


def edge_profiles(extent, members):
    place = np.arange(extent)
    whole_turn = 1.0 - ROOT ** (extent * members)
    rows = np.zeros((8, extent))
    rows[0] = KAPPA * ROOT**place / whole_turn
    rows[1] = -KAPPA * ROOT ** (extent - 1 - place) / whole_turn
    rows[2, 0] = DELTA
    rows[3, -1] = -DELTA
    return rows.astype(np.float32)


def split(values):
    high = values.astype(jnp.bfloat16)
    return high, (values - high.astype(jnp.float32)).astype(jnp.bfloat16)


def dot(left, right):
    return jnp.dot(left, right, preferred_element_type=jnp.float32)


def sums_kernel(u_ref, wx_ref, wy_ref, pair_ref, upper_ref, lower_ref, side_ref):
    step = pl.program_id(0)
    for plane in range(u_ref.shape[1]):
        u = u_ref[0, plane]
        slab = step * u_ref.shape[1] + plane
        along_x = jnp.dot(wx_ref[...], u, precision=HIGHEST, preferred_element_type=jnp.float32)
        for k in range(2):
            for target in (pair_ref, upper_ref, lower_ref):
                target[k, pl.ds(slab, 1), :] = along_x[k : k + 1]
        upper_ref[2, pl.ds(slab, 1), :] = along_x[2:3]
        lower_ref[2, pl.ds(slab, 1), :] = along_x[3:4]
        side_ref[0, plane] = lax.dot_general(
            wy_ref[...], u, (((1,), (1,)), ((), ())),
            precision=HIGHEST, preferred_element_type=jnp.float32,
        )


def second_kernel(u_ref, edge_ref, high_ref, low_ref, profile_ref, metric_ref, out_ref):
    planes, rows, columns = u_ref.shape[1:]
    u = u_ref[0].reshape(planes * rows, columns)
    u_high, u_low = split(u)
    total = dot(u_high, high_ref[...]) + dot(u_low, high_ref[...]) + dot(u_high, low_ref[...])
    metric = metric_ref[...]
    for plane in range(planes):
        edge = edge_ref[0, plane].T
        piece = total[plane * rows : (plane + 1) * rows]
        for k in range(4):
            piece = piece + edge[:, k : k + 1] * profile_ref[k : k + 1, :]
        out_ref[0, plane] = piece * metric


def first_kernel(u_ref, edge_ref, high_ref, low_ref, profile_ref, metric_ref, out_ref):
    planes = u_ref.shape[1]
    step = pl.program_id(0)
    left = jnp.concatenate([high_ref[...], high_ref[...], low_ref[...]], axis=1)
    metric = metric_ref[...]
    for plane in range(planes):
        u_high, u_low = split(u_ref[0, plane])
        total = dot(left, jnp.concatenate([u_high, u_low, u_high], axis=0))
        slab = step * planes + plane
        for k in range(4):
            total = total + profile_ref[:, k : k + 1] * edge_ref[k, pl.ds(slab, 1), :]
        out_ref[0, plane] = total * metric


def moved(block, axis, distance):
    count = lax.axis_size(axis)
    return lax.ppermute(block, axis, [(i, (i + distance) % count) for i in range(count)])


def whole(shape):
    return pl.BlockSpec(shape, lambda f: (0,) * len(shape))


def shards(fields, metric_first, metric_second):
    count, planes, rows, columns = fields.shape
    slabs = count * planes
    gx, gy = lax.axis_size("gx"), lax.axis_size("gy")
    slab_spec = pl.BlockSpec((1, planes, rows, columns), lambda f: (f, 0, 0, 0))
    params = pltpu.CompilerParams(vmem_limit_bytes=40 * MIB)
    size = fields.size
    shape = jax.ShapeDtypeStruct
    f32 = jnp.float32

    pair, upper, lower, side = pl.pallas_call(
        sums_kernel,
        grid=(count,),
        in_specs=[slab_spec, whole((8, rows)), whole((8, columns))],
        out_specs=[
            whole((2, slabs, columns)),
            whole((3, slabs, columns)),
            whole((3, slabs, columns)),
            pl.BlockSpec((1, planes, 8, rows), lambda f: (f, 0, 0, 0)),
        ],
        out_shape=[
            shape((2, slabs, columns), f32),
            shape((3, slabs, columns), f32),
            shape((3, slabs, columns), f32),
            shape((count, planes, 8, rows), f32),
        ],
        compiler_params=params,
        cost_estimate=pl.CostEstimate(flops=32 * size, bytes_accessed=4 * size, transcendentals=0),
    )(fields, sum_weights(rows), sum_weights(columns))

    sides = [moved(side[:, :, :4], "gy", q) for q in range(1, gy)] + [side[:, :, :4]]
    up = moved(upper, "gx", 1)
    down = moved(lower, "gx", -1)
    pairs = [up] + [moved(pair, "gx", q) for q in range(2, gx - 1)] + [down, pair]

    factor = np.float32(ROOT**columns)
    below, above = sides[gy - 1][:, :, 0], sides[gy - 1][:, :, 1]
    for q in range(gy - 1, 0, -1):
        below = sides[q - 1][:, :, 0] + factor * below
        above = sides[gy - q - 1][:, :, 1] + factor * above
    blank = jnp.zeros_like(below)
    edge_second = jnp.stack(
        [below, above, sides[0][:, :, 2], sides[gy - 2][:, :, 3]] + [blank] * 4, axis=2
    )

    high, low = piece_matrix(columns)
    slope_second = pl.pallas_call(
        second_kernel,
        grid=(count,),
        in_specs=[
            slab_spec,
            pl.BlockSpec((1, planes, 8, rows), lambda f: (f, 0, 0, 0)),
            whole((columns, columns)),
            whole((columns, columns)),
            whole((8, columns)),
            whole((1, columns)),
        ],
        out_specs=slab_spec,
        out_shape=shape(fields.shape, f32),
        compiler_params=params,
        cost_estimate=pl.CostEstimate(
            flops=6 * size * columns, bytes_accessed=8 * size, transcendentals=0
        ),
    )(
        fields, edge_second, np.ascontiguousarray(high.T), np.ascontiguousarray(low.T),
        edge_profiles(columns, gy), metric_second[None, :],
    )

    factor = np.float32(ROOT**rows)
    below, above = pairs[gx - 1][0], pairs[gx - 1][1]
    for q in range(gx - 1, 0, -1):
        below = pairs[q - 1][0] + factor * below
        above = pairs[gx - q - 1][1] + factor * above
    edge_first = jnp.stack([below, above, up[2], down[2]])

    high, low = piece_matrix(rows)
    slope_first = pl.pallas_call(
        first_kernel,
        grid=(count,),
        in_specs=[
            slab_spec,
            whole((4, slabs, columns)),
            whole((rows, rows)),
            whole((rows, rows)),
            whole((rows, 8)),
            whole((rows, 1)),
        ],
        out_specs=slab_spec,
        out_shape=shape(fields.shape, f32),
        compiler_params=params,
        cost_estimate=pl.CostEstimate(
            flops=6 * size * rows, bytes_accessed=8 * size, transcendentals=0
        ),
    )(
        fields, edge_first, high, low,
        np.ascontiguousarray(edge_profiles(rows, gx).T), metric_first[:, None],
    )
    return slope_first, slope_second


def solution(mesh):
    placed = (P(None, None, "gx", "gy"), P("gx"), P("gy"))
    return jax.shard_map(
        shards,
        mesh=mesh,
        in_specs=placed,
        out_specs=(P(None, None, "gx", "gy"), P(None, None, "gx", "gy")),
        check_vma=False,
    )
```

```python
import jax
import jax.numpy as jnp
import ml_dtypes
import numpy as np
from jax import lax
from jax.experimental import pallas as pl
from jax.experimental.pallas import tpu as pltpu
from jax.sharding import PartitionSpec as P

ALPHA = 0.47
HALF_A = (ALPHA + 2.0) / 3.0
QUARTER_B = (4.0 * ALPHA - 1.0) / 12.0

ROOT = (-1.0 + np.sqrt(1.0 - 4.0 * ALPHA * ALPHA)) / (2.0 * ALPHA)
GAIN = 1.0 / (1.0 + 2.0 * ALPHA * ROOT)
KAPPA = GAIN * (HALF_A * (ROOT - 1.0 / ROOT) + QUARTER_B * (ROOT**2 - ROOT**-2))
DELTA = GAIN * QUARTER_B * (1.0 / ROOT - ROOT)

MIB = 1 << 20


def piece_matrix(extent):
    place = np.arange(extent)
    gap = place[:, None] - place[None, :]
    size = np.abs(gap)
    whole = np.sign(gap) * (KAPPA * ROOT**size + np.where(size == 1, DELTA, 0.0))
    high = whole.astype(ml_dtypes.bfloat16)
    low = (whole - high.astype(np.float64)).astype(ml_dtypes.bfloat16)
    return high, low


def sum_weights(extent):
    place = np.arange(extent)
    return np.stack([ROOT ** (extent - place), ROOT ** (place + 1)]).astype(np.float32)


def edge_profiles(extent, members):
    place = np.arange(extent)
    whole_turn = 1.0 - ROOT ** (extent * members)
    rows = np.zeros((8, extent))
    rows[0] = KAPPA * ROOT**place / whole_turn
    rows[1] = -KAPPA * ROOT ** (extent - 1 - place) / whole_turn
    rows[2, 0] = DELTA
    rows[3, -1] = -DELTA
    return rows.astype(np.float32)


def split(values):
    high = values.astype(jnp.bfloat16)
    return high, (values - high.astype(jnp.float32)).astype(jnp.bfloat16)


def dot(left, right):
    return jnp.dot(left, right, preferred_element_type=jnp.float32)


LAST, UP, DOWN, FIRST = range(4)


def partners(axis):
    count = lax.axis_size(axis)
    me = lax.axis_index(axis)
    return [(q, {axis: lax.rem(me + q, count)}) for q in range(1, count)]


def reach(own, arrived, factor):
    count = arrived.shape[0]
    below, above = own[UP], own[DOWN]
    for q in range(count - 1, 0, -1):
        below = arrived[q, UP] + factor * below
        above = arrived[count - q, DOWN] + factor * above
    return below, above, arrived[1, LAST], arrived[count - 1, FIRST]


def solve_kernel(
    u_ref, wx_ref, wy_ref, xh_ref, xl_ref, yh_ref, yl_ref,
    first_ref, second_ref, edge_x_ref, edge_y_ref,
    own_x, own_y, far_x, far_y, send_x, got_x, send_y, got_y,
):
    slabs, rows, columns = u_ref.shape
    padded = own_x.shape[1]
    along_x, along_y = partners("gx"), partners("gy")
    mesh_id = pl.DeviceIdType.MESH

    barrier = pltpu.get_barrier_semaphore()
    for _, device in along_x + along_y:
        pl.semaphore_signal(barrier, inc=1, device_id=device, device_id_type=mesh_id)

    own_x[...] = jnp.zeros_like(own_x)
    lane = lax.broadcasted_iota(jnp.int32, (rows, 128), 1)

    def sums(slab, gathered):
        u = u_ref[slab]
        own_x[LAST, pl.ds(slab, 1), :] = u[rows - 1 :]
        own_x[UP, pl.ds(slab, 1), :] = jnp.sum(u * wx_ref[:, 0:1], axis=0, keepdims=True)
        own_x[DOWN, pl.ds(slab, 1), :] = jnp.sum(u * wx_ref[:, 1:2], axis=0, keepdims=True)
        own_x[FIRST, pl.ds(slab, 1), :] = u[0:1]
        ends = (
            u[:, columns - 1 :],
            jnp.sum(u * wy_ref[0:1, :], axis=1, keepdims=True),
            jnp.sum(u * wy_ref[1:2, :], axis=1, keepdims=True),
            u[:, 0:1],
        )
        for k in range(4):
            gathered = jnp.where(lane == k * padded + slab, ends[k], gathered)
        return gathered

    gathered = lax.fori_loop(0, slabs, sums, jnp.zeros((rows, 128), jnp.float32)).T
    for k in range(4):
        own_y[k] = gathered[k * padded : (k + 1) * padded]

    pl.semaphore_wait(barrier, len(along_x) + len(along_y))
    copies = []
    for q, device in along_y:
        copies.append(pltpu.make_async_remote_copy(
            src_ref=own_y, dst_ref=far_y.at[q], send_sem=send_y.at[q], recv_sem=got_y.at[q],
            device_id=device, device_id_type=mesh_id,
        ))
    for q, device in along_x:
        low = LAST if q == 1 else UP
        high = FIRST if q == len(along_x) else DOWN
        part = pl.ds(low, high - low + 1)
        copies.append(pltpu.make_async_remote_copy(
            src_ref=own_x.at[part], dst_ref=far_x.at[q, part],
            send_sem=send_x.at[q], recv_sem=got_x.at[q],
            device_id=device, device_id_type=mesh_id,
        ))
    for copy in copies:
        copy.start()

    group = 3 if slabs % 3 == 0 else 1

    def multiply(step, carry):
        wide = jnp.concatenate([xh_ref[...], xh_ref[...], xl_ref[...]], axis=1)
        u = u_ref[pl.ds(step * group, group)]
        u_high, u_low = split(u)
        flat_high = u_high.reshape(group * rows, columns)
        flat_low = u_low.reshape(group * rows, columns)
        total = dot(flat_high, yh_ref[...]) + dot(flat_low, yh_ref[...]) + dot(flat_high, yl_ref[...])
        second_ref[pl.ds(step * group, group)] = total.reshape(group, rows, columns)
        for k in range(group):
            stack = jnp.concatenate([u_high[k], u_low[k], u_high[k]], axis=0)
            first_ref[step * group + k] = dot(wide, stack)
        return carry

    lax.fori_loop(0, slabs // group, multiply, 0)

    for copy in copies:
        copy.wait()
    for out, own, far, extent in (
        (edge_x_ref, own_x, far_x, rows), (edge_y_ref, own_y, far_y, columns),
    ):
        for k, values in enumerate(reach(own, far, np.float32(ROOT**extent))):
            out[k] = values


def finish_kernel(
    first_ref, second_ref, edge_x_ref, edge_y_ref, px_ref, py_ref, mx_ref, my_ref,
    slope_x_ref, slope_y_ref,
):
    planes = first_ref.shape[0]
    step = pl.program_id(0)
    for plane in range(planes):
        slab = step * planes + plane
        total = first_ref[plane]
        for k in range(4):
            total = total + px_ref[:, k : k + 1] * edge_x_ref[k, pl.ds(slab, 1), :]
        slope_x_ref[0, plane] = total * mx_ref[...]
        edges = [edge_y_ref[k, pl.ds(slab, 1), :] for k in range(4)]
        edge = jnp.concatenate(edges + edges, axis=0).T
        total = second_ref[plane]
        for k in range(4):
            total = total + edge[:, k : k + 1] * py_ref[k : k + 1, :]
        slope_y_ref[0, plane] = total * my_ref[...]


def whole(shape):
    return pl.BlockSpec(shape, lambda f: (0,) * len(shape))


def shards(fields, metric_first, metric_second):
    count, planes, rows, columns = fields.shape
    slabs = count * planes
    padded = -(-slabs // 8) * 8
    gx, gy = lax.axis_size("gx"), lax.axis_size("gy")
    size = fields.size
    f32 = jnp.float32
    shape = jax.ShapeDtypeStruct
    in_vmem = pl.BlockSpec(memory_space=pltpu.VMEM)

    x_high, x_low = piece_matrix(rows)
    y_high, y_low = (np.ascontiguousarray(part.T) for part in piece_matrix(columns))
    total_first, total_second, edge_x, edge_y = pl.pallas_call(
        solve_kernel,
        in_specs=[in_vmem] * 7,
        out_specs=[in_vmem] * 4,
        out_shape=[
            shape((slabs, rows, columns), f32),
            shape((slabs, rows, columns), f32),
            shape((4, padded, columns), f32),
            shape((4, padded, rows), f32),
        ],
        scratch_shapes=[
            pltpu.VMEM((4, padded, columns), f32),
            pltpu.VMEM((4, padded, rows), f32),
            pltpu.VMEM((gx, 4, padded, columns), f32),
            pltpu.VMEM((gy, 4, padded, rows), f32),
            pltpu.SemaphoreType.DMA((gx,)),
            pltpu.SemaphoreType.DMA((gx,)),
            pltpu.SemaphoreType.DMA((gy,)),
            pltpu.SemaphoreType.DMA((gy,)),
        ],
        compiler_params=pltpu.CompilerParams(
            collective_id=0, has_side_effects=True, vmem_limit_bytes=40 * MIB
        ),
        cost_estimate=pl.CostEstimate(
            flops=6 * size * (rows + columns), bytes_accessed=4 * size, transcendentals=0
        ),
    )(
        fields.reshape(slabs, rows, columns),
        np.ascontiguousarray(sum_weights(rows).T), sum_weights(columns),
        x_high, x_low, y_high, y_low,
    )

    total_spec = pl.BlockSpec((planes, rows, columns), lambda f: (f, 0, 0))
    slope_spec = pl.BlockSpec((1, planes, rows, columns), lambda f: (f, 0, 0, 0))
    return pl.pallas_call(
        finish_kernel,
        grid=(count,),
        in_specs=[
            total_spec,
            total_spec,
            whole((4, padded, columns)),
            whole((4, padded, rows)),
            whole((rows, 8)),
            whole((8, columns)),
            whole((rows, 1)),
            whole((1, columns)),
        ],
        out_specs=[slope_spec, slope_spec],
        out_shape=[shape(fields.shape, f32)] * 2,
        compiler_params=pltpu.CompilerParams(vmem_limit_bytes=24 * MIB),
        cost_estimate=pl.CostEstimate(flops=20 * size, bytes_accessed=16 * size, transcendentals=0),
    )(
        total_first, total_second, edge_x, edge_y,
        np.ascontiguousarray(edge_profiles(rows, gx).T), edge_profiles(columns, gy),
        metric_first[:, None], metric_second[None, :],
    )


def solution(mesh):
    placed = (P(None, None, "gx", "gy"), P("gx"), P("gy"))
    return jax.shard_map(
        shards,
        mesh=mesh,
        in_specs=placed,
        out_specs=(P(None, None, "gx", "gy"), P(None, None, "gx", "gy")),
        check_vma=False,
    )
```

```python
import functools

import jax
import jax.numpy as jnp
import ml_dtypes
import numpy as np
from jax import lax
from jax.experimental import pallas as pl
from jax.experimental.pallas import tpu as pltpu
from jax.sharding import PartitionSpec as P

ALPHA = 0.47
HALF_A = (ALPHA + 2.0) / 3.0
QUARTER_B = (4.0 * ALPHA - 1.0) / 12.0

ROOT = (-1.0 + np.sqrt(1.0 - 4.0 * ALPHA * ALPHA)) / (2.0 * ALPHA)
GAIN = 1.0 / (1.0 + 2.0 * ALPHA * ROOT)
KAPPA = GAIN * (HALF_A * (ROOT - 1.0 / ROOT) + QUARTER_B * (ROOT**2 - ROOT**-2))
DELTA = GAIN * QUARTER_B * (1.0 / ROOT - ROOT)

MIB = 1 << 20


def piece_matrix(extent):
    place = np.arange(extent)
    gap = place[:, None] - place[None, :]
    size = np.abs(gap)
    whole = np.sign(gap) * (KAPPA * ROOT**size + np.where(size == 1, DELTA, 0.0))
    high = whole.astype(ml_dtypes.bfloat16)
    low = (whole - high.astype(np.float64)).astype(ml_dtypes.bfloat16)
    return high, low


def sum_weights(extent):
    place = np.arange(extent)
    return np.stack([ROOT ** (extent - place), ROOT ** (place + 1)]).astype(np.float32)


def over_lanes(rows):
    return np.ascontiguousarray(np.broadcast_to(rows[:, :, None], rows.shape + (128,)))


def edge_profiles(extent, members):
    place = np.arange(extent)
    whole_turn = 1.0 - ROOT ** (extent * members)
    rows = np.zeros((8, extent))
    rows[0] = KAPPA * ROOT**place / whole_turn
    rows[1] = -KAPPA * ROOT ** (extent - 1 - place) / whole_turn
    rows[2, 0] = DELTA
    rows[3, -1] = -DELTA
    return rows.astype(np.float32)


def split(values):
    high = values.astype(jnp.bfloat16)
    return high, (values - high.astype(jnp.float32)).astype(jnp.bfloat16)


def dot(left, right):
    return jnp.dot(left, right, preferred_element_type=jnp.float32)


LAST, UP, DOWN, FIRST = range(4)


def partners(axis):
    count = lax.axis_size(axis)
    me = lax.axis_index(axis)
    return [(q, {axis: lax.rem(me + q, count)}) for q in range(1, count)]


def reach(own, arrived, factor):
    count = arrived.shape[0]
    below, above = own[UP], own[DOWN]
    for q in range(count - 1, 0, -1):
        below = arrived[q, UP] + factor * below
        above = arrived[count - q, DOWN] + factor * above
    return below, above, arrived[1, LAST], arrived[count - 1, FIRST]


def solve_kernel(
    group, u_hbm, wx_hbm, wy_hbm, xh_hbm, xl_hbm, yh_hbm, yl_hbm,
    first_ref, second_ref, edge_x_ref, edge_y_ref,
    u_ref, wx_ref, wy_ref, xh_ref, xl_ref, yh_ref, yl_ref,
    own_x, own_y, far_x, far_y, u_sem, load_sem, send_x, got_x, send_y, got_y,
):
    slabs, rows, columns = u_ref.shape
    padded = own_x.shape[1]
    along_x, along_y = partners("gx"), partners("gy")
    mesh_id = pl.DeviceIdType.MESH

    def chunk(step):
        part = pl.ds(step * group, group)
        return pltpu.make_async_copy(u_hbm.at[part], u_ref.at[part], u_sem.at[step])

    constants = (
        (wx_hbm, wx_ref), (wy_hbm, wy_ref), (xh_hbm, xh_ref), (xl_hbm, xl_ref),
        (yh_hbm, yh_ref), (yl_hbm, yl_ref),
    )
    loads = [
        pltpu.make_async_copy(*pair, load_sem.at[k]) for k, pair in enumerate(constants)
    ]
    for load in loads[:2]:
        load.start()
    for step in range(slabs // group):
        chunk(step).start()
    for load in loads[2:]:
        load.start()

    barrier = pltpu.get_barrier_semaphore()
    for _, device in along_x + along_y:
        pl.semaphore_signal(barrier, inc=1, device_id=device, device_id_type=mesh_id)

    own_x[...] = jnp.zeros_like(own_x)
    lane = lax.broadcasted_iota(jnp.int32, (rows, 128), 1)

    def sums(slab, gathered):
        own_x[LAST, pl.ds(slab, 1), :] = u_ref[slab, rows - 1 :]
        own_x[FIRST, pl.ds(slab, 1), :] = u_ref[slab, 0:1]
        up, down, lines = 0.0, 0.0, ([], [])
        for at in range(0, columns, 128):
            u = u_ref[slab, :, at : at + 128]
            for k in range(2):
                lines[k].append(jnp.sum(u * wx_ref[k], axis=0, keepdims=True))
            up = up + u * wy_ref[0:1, at : at + 128]
            down = down + u * wy_ref[1:2, at : at + 128]
        own_x[UP, pl.ds(slab, 1), :] = jnp.concatenate(lines[0], axis=1)
        own_x[DOWN, pl.ds(slab, 1), :] = jnp.concatenate(lines[1], axis=1)
        ends = (
            u_ref[slab, :, columns - 128 :][:, 127:],
            jnp.sum(up, axis=1, keepdims=True),
            jnp.sum(down, axis=1, keepdims=True),
            u_ref[slab, :, :128][:, 0:1],
        )
        for k in range(4):
            gathered = jnp.where(lane == k * padded + slab, ends[k], gathered)
        return gathered

    def sums_of_chunk(step, gathered):
        chunk(step).wait()
        for k in range(group):
            gathered = sums(step * group + k, gathered)
        return gathered

    for load in loads[:2]:
        load.wait()
    gathered = lax.fori_loop(
        0, slabs // group, sums_of_chunk, jnp.zeros((rows, 128), jnp.float32)
    ).T
    for k in range(4):
        own_y[k] = gathered[k * padded : (k + 1) * padded]

    pl.semaphore_wait(barrier, len(along_x) + len(along_y))
    copies = []
    for q, device in along_y:
        copies.append(pltpu.make_async_remote_copy(
            src_ref=own_y, dst_ref=far_y.at[q], send_sem=send_y.at[q], recv_sem=got_y.at[q],
            device_id=device, device_id_type=mesh_id,
        ))
    for q, device in along_x:
        low = LAST if q == 1 else UP
        high = FIRST if q == len(along_x) else DOWN
        part = pl.ds(low, high - low + 1)
        copies.append(pltpu.make_async_remote_copy(
            src_ref=own_x.at[part], dst_ref=far_x.at[q, part],
            send_sem=send_x.at[q], recv_sem=got_x.at[q],
            device_id=device, device_id_type=mesh_id,
        ))
    for copy in copies:
        copy.start()

    for load in loads[2:]:
        load.wait()

    def multiply(step, carry):
        wide = jnp.concatenate([xh_ref[...], xh_ref[...], xl_ref[...]], axis=1)
        u = u_ref[pl.ds(step * group, group)]
        u_high, u_low = split(u)
        flat_high = u_high.reshape(group * rows, columns)
        flat_low = u_low.reshape(group * rows, columns)
        total = dot(flat_high, yh_ref[...]) + dot(flat_low, yh_ref[...]) + dot(flat_high, yl_ref[...])
        second_ref[pl.ds(step * group, group)] = total.reshape(group, rows, columns)
        for k in range(group):
            stack = jnp.concatenate([u_high[k], u_low[k], u_high[k]], axis=0)
            first_ref[step * group + k] = dot(wide, stack)
        return carry

    lax.fori_loop(0, slabs // group, multiply, 0)

    for copy in copies:
        copy.wait()
    for out, own, far, extent in (
        (edge_x_ref, own_x, far_x, rows), (edge_y_ref, own_y, far_y, columns),
    ):
        for k, values in enumerate(reach(own, far, np.float32(ROOT**extent))):
            out[k] = values


def finish_kernel(
    group, first_ref, second_ref, edge_x_ref, edge_y_ref, px_ref, py_ref, mx_ref, my_ref,
    x_hbm, y_hbm, x_ref, y_ref, x_sem, y_sem,
):
    slabs, rows, columns = first_ref.shape
    metric_column = jnp.broadcast_to(mx_ref[...], (8, rows)).T[:, 0:1]
    metric_wide = jnp.broadcast_to(metric_column, (rows, 128))

    def outward(step):
        part = pl.ds(step * group, group)
        return (
            pltpu.make_async_copy(x_ref.at[part], x_hbm.at[part], x_sem.at[step]),
            pltpu.make_async_copy(y_ref.at[part], y_hbm.at[part], y_sem.at[step]),
        )

    def finish(step, carry):
        to_x, to_y = outward(step)
        for k in range(group):
            slab = step * group + k
            edges = [edge_x_ref[k, pl.ds(slab, 1), :] for k in range(4)]
            for at in range(0, columns, 128):
                tile = slice(at, at + 128)
                total = first_ref[slab, :, tile]
                total = total + px_ref[0] * edges[0][:, tile] + px_ref[1] * edges[1][:, tile]
                x_ref[slab, :, tile] = total * metric_wide
            for row, value in ((0, DELTA * edges[2]), (rows - 1, -DELTA * edges[3])):
                at = pl.ds(row, 1)
                x_ref[slab, at, :] = x_ref[slab, at, :] + value * metric_column[row : row + 1]
        to_x.start()
        for k in range(group):
            slab = step * group + k
            edges = [edge_y_ref[k, pl.ds(slab, 1), :] for k in range(4)]
            edge = jnp.concatenate(edges + edges, axis=0).T
            for at in range(0, columns, 128):
                tile = slice(at, at + 128)
                total = second_ref[slab, :, tile]
                terms = [0, 1] + [2] * (at == 0) + [3] * (at == columns - 128)
                for k in terms:
                    total = total + edge[:, k : k + 1] * py_ref[k : k + 1, tile]
                y_ref[slab, :, tile] = total * my_ref[:, tile]
        to_y.start()
        return carry

    lax.fori_loop(0, slabs // group, finish, 0)

    def drain(step, carry):
        for copy in outward(step):
            copy.wait()
        return carry

    lax.fori_loop(0, slabs // group, drain, 0)


def shards(fields, metric_first, metric_second):
    count, planes, rows, columns = fields.shape
    slabs = count * planes
    padded = -(-slabs // 8) * 8
    gx, gy = lax.axis_size("gx"), lax.axis_size("gy")
    size = fields.size
    f32 = jnp.float32
    shape = jax.ShapeDtypeStruct
    in_vmem = pl.BlockSpec(memory_space=pltpu.VMEM)

    in_hbm = pl.BlockSpec(memory_space=pltpu.HBM)
    slab_shape = (slabs, rows, columns)

    x_high, x_low = piece_matrix(rows)
    y_high, y_low = (np.ascontiguousarray(part.T) for part in piece_matrix(columns))
    loaded = (
        over_lanes(sum_weights(rows)), sum_weights(columns), x_high, x_low, y_high, y_low
    )
    total_first, total_second, edge_x, edge_y = pl.pallas_call(
        functools.partial(solve_kernel, planes),
        in_specs=[in_hbm] * 7,
        out_specs=[in_vmem] * 4,
        out_shape=[
            shape(slab_shape, f32),
            shape(slab_shape, f32),
            shape((4, padded, columns), f32),
            shape((4, padded, rows), f32),
        ],
        scratch_shapes=[pltpu.VMEM(slab_shape, f32)]
        + [pltpu.VMEM(part.shape, part.dtype) for part in loaded]
        + [
            pltpu.VMEM((4, padded, columns), f32),
            pltpu.VMEM((4, padded, rows), f32),
            pltpu.VMEM((gx, 4, padded, columns), f32),
            pltpu.VMEM((gy, 4, padded, rows), f32),
            pltpu.SemaphoreType.DMA((count,)),
            pltpu.SemaphoreType.DMA((len(loaded),)),
            pltpu.SemaphoreType.DMA((gx,)),
            pltpu.SemaphoreType.DMA((gx,)),
            pltpu.SemaphoreType.DMA((gy,)),
            pltpu.SemaphoreType.DMA((gy,)),
        ],
        compiler_params=pltpu.CompilerParams(
            collective_id=0, has_side_effects=True, vmem_limit_bytes=40 * MIB
        ),
        cost_estimate=pl.CostEstimate(
            flops=6 * size * (rows + columns), bytes_accessed=4 * size, transcendentals=0
        ),
    )(*(
        pltpu.with_memory_space_constraint(part, pltpu.HBM)
        for part in (fields.reshape(slab_shape), *map(jnp.asarray, loaded))
    ))

    slope_first, slope_second = pl.pallas_call(
        functools.partial(finish_kernel, planes),
        in_specs=[in_vmem] * 8,
        out_specs=[in_hbm] * 2,
        out_shape=[shape(slab_shape, f32)] * 2,
        scratch_shapes=[
            pltpu.VMEM(slab_shape, f32),
            pltpu.VMEM(slab_shape, f32),
            pltpu.SemaphoreType.DMA((count,)),
            pltpu.SemaphoreType.DMA((count,)),
        ],
        compiler_params=pltpu.CompilerParams(vmem_limit_bytes=36 * MIB),
        cost_estimate=pl.CostEstimate(flops=20 * size, bytes_accessed=16 * size, transcendentals=0),
    )(
        total_first, total_second, edge_x, edge_y,
        over_lanes(edge_profiles(rows, gx)[:2]), edge_profiles(columns, gy),
        metric_first[None, :], metric_second[None, :],
    )
    return slope_first.reshape(fields.shape), slope_second.reshape(fields.shape)


def solution(mesh):
    placed = (P(None, None, "gx", "gy"), P("gx"), P("gy"))
    return jax.shard_map(
        shards,
        mesh=mesh,
        in_specs=placed,
        out_specs=(P(None, None, "gx", "gy"), P(None, None, "gx", "gy")),
        check_vma=False,
    )
```
